32 devices in a mesh: train: 8 (over z, y), test: 4 (over x, core).
Axes of the slice: x: 2, y: 2, z: 4, core: 2. Of those that a mesh axis runs over, the one named last changes fastest.
Arguments:
- query_out: bfloat16 [2048, 3584], P('train', 'test'), may hold values from -16 to 16, as said below
- query_in: bfloat16 [2048, 3584], P('train', 'test'), may hold values from -6 to 6
- passage_out: bfloat16 [2048, 3584], P('train', 'test'), may hold values from -16 to 16, as said below
- passage_in_sum: bfloat16 [2048, 3584], P('train', 'test'), may hold values from -192 to 192
- passage_len: int32 [2048], P('train'), may hold values from 16 to 512
- positive: int32 [2048], P('train'), may hold values from 0 to 2047
- proj_in: bfloat16 [3584, 64], P('test'), may hold values from -0.09375 to 0.09375
- proj_out: bfloat16 [3584, 64], P('test'), may hold values from -0.09375 to 0.09375
- test_grads: bfloat16 [2048, 4096], P(('test', 'train')), may hold values from -6 to 6
Outputs:
- scores: float32 [2048, 2048], P('train', 'test')
The draws below stay inside these ranges and needn't reach their ends.
Inputs may be any that keep to these rules, and one draw needn't show every extreme that they name: `query_out`: entries stay within the range. `passage_out`: entries stay within the range.
All inputs are finite; a program needn't handle non-finite values.
Results may differ from the reference program's by a relative error of at most 0.0034.
Values may be sent and summed in bfloat16 or wider, within the bound.
No kernel may reach another device: no remote copies, remote signals or barrier semaphores. Data moves between devices by JAX's collectives and lax.ppermute only.
A program may use at most 64 MiB of HBM per device.

```python
import math
import jax
import jax.numpy as jnp
from jax import lax

D = 3584
RANK = 64
PROJ = 4096
BATCH = 2048
NTEST = 2048


def draw_embeddings(key):
    keys = jax.random.split(jax.random.fold_in(key, 7), 6)
    queries = jax.random.normal(keys[0], (BATCH, D), jnp.float32)
    passages = jax.random.normal(keys[1], (BATCH, D), jnp.float32)
    chosen = jnp.arange(16, dtype=jnp.int32) * (BATCH // 16) + jax.random.randint(keys[4], (16,), 0, BATCH // 16)
    targets = (chosen + BATCH // 2) % BATCH
    second = (targets + 1) % BATCH
    target_logit = jnp.tile(jnp.array([120.0, 180.0, 240.0, 320.0], jnp.float32), 4)[:, None]
    strength = jnp.sqrt(target_logit) / float(D) ** 0.25
    shared = jnp.clip(jax.random.normal(keys[5], (16, D), jnp.float32), -2.5, 2.5) * strength
    queries = queries.at[chosen].set(shared)
    passages = passages.at[targets].set(shared)
    passages = passages.at[second].set(0.99 * shared)
    return (jnp.clip(queries, -16.0, 16.0), jnp.clip(passages, -16.0, 16.0))


def draw_query_out(key, part):
    return draw_embeddings(key)[0].astype(jnp.bfloat16)


def draw_passage_out(key, part):
    return draw_embeddings(key)[1].astype(jnp.bfloat16)


def with_ends(drawn, rng, smallest, high):
    shape = drawn.shape
    index_at = [jax.random.randint(jax.random.fold_in(rng, axis), (), 0, shape[axis]) for axis in range(len(shape))]
    drawn = drawn.at[tuple(index_at)].set(smallest)
    longest = shape.index(max(shape))
    index_at[longest] = (index_at[longest] + 1) % shape[longest]
    return drawn.at[tuple(index_at)].set(high)


def level_of(key, shape, pieces, least, high):
    gain, own = 1.0, jax.random.fold_in(key, 6)
    for axis_at, parts in pieces:
        steps = jnp.exp(jax.random.uniform(jax.random.fold_in(own, axis_at), (parts,), jnp.float32, least / len(pieces), high / len(pieces)))
        gain = gain * jnp.repeat(steps, shape[axis_at] // parts).reshape([-1 if axis == axis_at else 1 for axis in range(len(shape))])
    return gain


def gaussian(own_key, dims, spread, limit, pieces=(), kind=jnp.bfloat16):
    gain = level_of(own_key, dims, pieces, -0.22, 0.18) if pieces else 1.0
    values = jax.random.normal(own_key, dims, jnp.float32) * spread * gain
    return jnp.minimum(jnp.maximum(values, -limit), limit).astype(kind)


def setup_inputs(seed: int = 0) -> dict:
    key_of = jax.random.split(jax.random.key(seed), 10)
    query_out = draw_query_out(jax.random.fold_in(key_of[9], 71), 0)
    query_in = gaussian(key_of[1], (BATCH, D), 1.0, 6.0, ((0, 8), (1, 4)))
    passage_out = draw_passage_out(jax.random.fold_in(key_of[9], 71), 0)
    passage_in_sum = gaussian(key_of[3], (BATCH, D), 32.0, 192.0, ((0, 8), (1, 4)))
    passage_len = with_ends(jax.random.randint(key_of[4], (BATCH,), 16, 513), jax.random.fold_in(key_of[4], 1), 16, 512).astype(jnp.int32)
    positive = with_ends(jax.random.randint(key_of[5], (BATCH,), 0, BATCH), jax.random.fold_in(key_of[5], 1), 0, BATCH - 1).astype(jnp.int32)
    proj_in = gaussian(key_of[6], (D, RANK), D ** -0.5, 0.09375, ((0, 4),))
    proj_out = gaussian(key_of[7], (D, RANK), D ** -0.5, 0.09375, ((0, 4),))
    test_grads = gaussian(key_of[8], (NTEST, PROJ), 1.0, 6.0, ((0, 32),))
    return dict(query_out=query_out, query_in=query_in, passage_out=passage_out, passage_in_sum=passage_in_sum, passage_len=passage_len, positive=positive, proj_in=proj_in, proj_out=proj_out, test_grads=test_grads)


def reference(query_out, query_in, passage_out, passage_in_sum, passage_len, positive, proj_in, proj_out, test_grads):
    logit_scale = 1.0 / math.sqrt(D)
    logits = jnp.dot(query_out, passage_out.T, preferred_element_type=jnp.float32) * logit_scale
    row_top = lax.optimization_barrier(jnp.max(logits, axis=1, keepdims=True))
    exp_terms = jnp.exp(logits - row_top)
    prob = exp_terms / lax.optimization_barrier(jnp.sum(exp_terms, axis=1, keepdims=True))
    columns = jnp.arange(BATCH, dtype=jnp.int32)
    is_positive = (columns[None, :] == positive[:, None]).astype(jnp.float32)
    dlogit = (prob - is_positive).astype(jnp.bfloat16)
    grad_query = jnp.dot(dlogit, passage_out, preferred_element_type=jnp.float32) * logit_scale
    grad_pass = jnp.dot(dlogit.T, query_out, preferred_element_type=jnp.float32) * logit_scale
    proj_wide = proj_out.astype(jnp.float32)
    act_query = jnp.dot(query_in, proj_in, preferred_element_type=jnp.float32)
    act_pass = jnp.dot(passage_in_sum, proj_in, preferred_element_type=jnp.float32) / passage_len[:, None].astype(jnp.float32)
    out_query = jnp.dot(grad_query, proj_wide, precision=lax.Precision.HIGHEST)
    out_pass = jnp.dot(grad_pass, proj_wide, precision=lax.Precision.HIGHEST)
    train_grads = act_query[:, :, None] * out_query[:, None, :] + act_pass[:, :, None] * out_pass[:, None, :]
    train_grads = train_grads.reshape(BATCH, RANK * RANK).astype(jnp.bfloat16)
    return jnp.dot(train_grads, test_grads.T, preferred_element_type=jnp.float32)
```

```python
import math

import jax
import jax.numpy as jnp
from jax import lax
from jax.sharding import PartitionSpec as P

D = 3584
F32 = jnp.float32
BF16 = jnp.bfloat16


def dot(a, b, ca, cb):
    return lax.dot_general(a, b, (((ca,), (cb,)), ((), ())), preferred_element_type=F32)


def split_two(a):
    high = a.astype(BF16)
    rest = (a - high.astype(F32)).astype(BF16)
    return jnp.concatenate((high, rest), axis=0)


def local(
    n_train,
    n_test,
    query_out,
    query_in,
    passage_out,
    passage_in_sum,
    passage_len,
    positive,
    proj_in,
    proj_out,
    test_grads,
):
    rank = proj_in.shape[1]
    rows = query_out.shape[0]
    tests = test_grads.shape[0]
    scale = 1.0 / math.sqrt(D)
    me_train = lax.axis_index("train")
    me_test = lax.axis_index("test")
    core = lax.rem(me_test, 2)
    seg_at = lax.div(me_test, 2)
    segs = n_test // 2
    seg = rows // segs
    half = rows // 2
    near = 2
    far = [1 << i for i in range(n_train.bit_length() - 1) if (1 << i) != near]

    def over_train(a, bit):
        return lax.ppermute(a, "train", [(i, i ^ bit) for i in range(n_train)])

    def over_test(a, bit):
        return lax.ppermute(a, "test", [(i, i ^ bit) for i in range(n_test)])

    def gather_far(own):
        held = {0: own}
        for bit in reversed(far):
            held.update({mask | bit: over_train(a, bit) for mask, a in list(held.items())})
        return held

    masks = [0]
    for bit in far:
        masks = masks + [mask | bit for mask in masks]
    n_far = len(masks)

    passages = gather_far(passage_out)
    query_near = over_train(query_out, near)

    factors = jnp.concatenate(
        (
            dot(proj_in, query_in, 0, 1),
            dot(proj_in, passage_in_sum, 0, 1),
            dot(proj_out, query_out, 0, 1),
            dot(proj_out, passage_out, 0, 1),
        ),
        axis=0,
    )
    bit = 1
    while bit < n_test:
        factors = factors + over_test(factors, bit)
        bit *= 2

    queries = jnp.stack((query_out, query_near)).reshape(2, segs, seg, -1)
    queries = queries.transpose(1, 0, 2, 3).reshape(2 * rows, -1)

    def summed_logits(blocks):
        mine = jnp.concatenate(
            [lax.dynamic_slice_in_dim(b, core * half, half, 0) for b in blocks], axis=0
        )
        theirs = jnp.concatenate(
            [lax.dynamic_slice_in_dim(b, (1 - core) * half, half, 0) for b in blocks], axis=0
        )
        sent = over_test(dot(theirs, queries, 1, 1), 1)
        total = dot(mine, queries, 1, 1) + sent
        width = 2 * rows
        bit = n_test // 2
        while bit > 1:
            width //= 2
            upper = lax.rem(lax.div(me_test, bit), 2)
            keep = lax.dynamic_slice_in_dim(total, upper * width, width, 1)
            give = lax.dynamic_slice_in_dim(total, (1 - upper) * width, width, 1)
            total = keep + over_test(give, bit)
            bit //= 2
        return total

    logits = (
        jnp.concatenate(
            [
                summed_logits([passages[m] for m in masks[: n_far // 2]]),
                summed_logits([passages[m] for m in masks[n_far // 2 :]]),
            ],
            axis=0,
        )
        * scale
    )

    def swap(a):
        return jnp.concatenate((a[:, seg:], a[:, :seg]), axis=1)

    top = jnp.max(logits, axis=0, keepdims=True)
    total = jnp.sum(jnp.exp(logits - top), axis=0, keepdims=True)

    def merge(top, total, other):
        new_top = jnp.maximum(top, other[:1])
        return new_top, total * jnp.exp(top - new_top) + other[1:] * jnp.exp(other[:1] - new_top)

    top, total = merge(top, total, over_test(jnp.concatenate((top, total), axis=0), 1))
    top, total = merge(
        top, total, over_train(swap(jnp.concatenate((top, total), axis=0)), near)
    )
    positive_own = positive[None, :]
    positive_near = over_train(positive_own, near)
    wanted = jnp.concatenate(
        [lax.dynamic_slice_in_dim(a, seg_at * seg, seg, 1) for a in (positive_own, positive_near)],
        axis=1,
    )
    columns = jnp.concatenate(
        [
            lax.broadcasted_iota(jnp.int32, (half, 1), 0)
            + ((me_train ^ mask) * rows + core * half)
            for mask in masks
        ],
        axis=0,
    )
    prob = jnp.exp(logits - top) / total
    dlogit = (prob - (columns == wanted).astype(F32)).astype(BF16)

    pass_small = gather_far(
        lax.dynamic_slice_in_dim(factors[3 * rank :], core * half, half, 1)
    )
    pass_small = jnp.concatenate([pass_small[m] for m in masks], axis=1)
    factors_near = over_train(factors[: 3 * rank], near)
    query_small = jnp.concatenate(
        [
            lax.dynamic_slice_in_dim(a[2 * rank : 3 * rank], seg_at * seg, seg, 1)
            for a in (factors, factors_near)
        ],
        axis=1,
    )

    out_query = dot(split_two(pass_small), dlogit, 1, 0)
    out_query = (out_query[:rank] + out_query[rank:]) * scale
    out_pass = dot(split_two(query_small), dlogit, 1, 1)
    out_pass = (out_pass[:rank] + out_pass[rank:]) * scale

    for bit in reversed(far):
        width = out_pass.shape[1] // 2
        out_pass = out_pass[:, :width] + over_train(out_pass[:, width:], bit)
    bit = 2
    while bit < n_test:
        out_pass = out_pass + over_test(out_pass, bit)
        bit *= 2
    out_pass = jnp.concatenate((out_pass, over_train(out_pass, near)), axis=0)
    out_pass_other = over_test(out_pass, 1)
    out_pass = jnp.where(
        core == 0,
        jnp.concatenate((out_pass, out_pass_other), axis=1),
        jnp.concatenate((out_pass_other, out_pass), axis=1),
    )

    out_query = out_query + over_test(out_query, 1)
    out_query = out_query + over_train(swap(out_query), near)
    out_query = jnp.concatenate((out_query[:, :seg], out_query[:, seg:]), axis=0)
    bit = 2
    while bit < n_test:
        other = over_test(out_query, bit)
        out_query = jnp.where(
            lax.rem(lax.div(me_test, bit), 2) == 0,
            jnp.concatenate((out_query, other), axis=1),
            jnp.concatenate((other, out_query), axis=1),
        )
        bit *= 2

    held = gather_far(test_grads)
    test_block = jnp.zeros((n_far * tests, test_grads.shape[1]), BF16)
    for mask in masks:
        owner = me_train ^ mask
        at = lax.div(owner, 2 * near) * near + lax.rem(owner, near)
        test_block = lax.dynamic_update_slice_in_dim(test_block, held[mask], at * tests, 0)

    lens = passage_len[None, :].astype(F32)
    act_query = (factors[:rank], factors_near[:rank])
    act_pass = (
        factors[rank : 2 * rank] / lens,
        factors_near[rank : 2 * rank] / over_train(passage_len[None, :], near).astype(F32),
    )

    def scores_of(which):
        oq = out_query[which * rank : (which + 1) * rank]
        op = out_pass[which * rank : (which + 1) * rank]
        outer = (
            act_query[which][:, None, :] * oq[None, :, :]
            + act_pass[which][:, None, :] * op[None, :, :]
        )
        grads = outer.reshape(rank * rank, rows).astype(BF16)
        return dot(grads, test_block, 0, 1)

    given = over_train(scores_of(1), near)
    mine = scores_of(0)
    unit = near * tests
    mine = [mine[:, i : i + unit] for i in range(0, mine.shape[1], unit)]
    given = [given[:, i : i + unit] for i in range(0, given.shape[1], unit)]
    upper = lax.rem(lax.div(me_train, near), 2) == 1
    pieces = []
    for a, b in zip(mine, given):
        pieces += [jnp.where(upper, b, a), jnp.where(upper, a, b)]
    return jnp.concatenate(pieces, axis=1)


def solution(mesh):
    def body(*args):
        return local(mesh.shape["train"], mesh.shape["test"], *args)

    return jax.shard_map(
        body,
        mesh=mesh,
        in_specs=(
            P("train", "test"),
            P("train", "test"),
            P("train", "test"),
            P("train", "test"),
            P("train"),
            P("train"),
            P("test", None),
            P("test", None),
            P(("test", "train"), None),
        ),
        out_specs=P("train", "test"),
        check_vma=False,
    )
```

```python
import math

import jax
import jax.numpy as jnp
from jax import lax
from jax.sharding import PartitionSpec as P

D = 3584
F32 = jnp.float32
BF16 = jnp.bfloat16


def dot(a, b, ca, cb):
    return lax.dot_general(a, b, (((ca,), (cb,)), ((), ())), preferred_element_type=F32)


def split_two(a):
    high = lax.reduce_precision(a, exponent_bits=8, mantissa_bits=7)
    return jnp.concatenate((high.astype(BF16), (a - high).astype(BF16)), axis=0)


def after(a, *others):
    return lax.optimization_barrier((a, *others))[0]


def local(
    n_train,
    n_test,
    query_out,
    query_in,
    passage_out,
    passage_in_sum,
    passage_len,
    positive,
    proj_in,
    proj_out,
    test_grads,
):
    rank = proj_in.shape[1]
    rows, feats = query_out.shape
    tests = test_grads.shape[0]
    scale = 1.0 / math.sqrt(D)
    me_train = lax.axis_index("train")
    me_test = lax.axis_index("test")
    core = lax.rem(me_test, 2)
    seg_at = lax.div(me_test, 2)
    segs = n_test // 2
    seg = rows // segs
    half = rows // 2
    near = 2
    high_bits = [1 << i for i in range(2, n_train.bit_length() - 1)]
    far = high_bits + [1]

    def over_train(a, bit):
        return lax.ppermute(a, "train", [(i, i ^ bit) for i in range(n_train)])

    def over_test(a, bit):
        return lax.ppermute(a, "test", [(i, i ^ bit) for i in range(n_test)])

    def gather(held, bits):
        held = dict(held)
        for bit in reversed(bits):
            held.update({mask | bit: over_train(a, bit) for mask, a in list(held.items())})
        return held

    masks = [0]
    for bit in far:
        masks = masks + [mask | bit for mask in masks]
    n_far = len(masks)

    halves = passage_out.reshape(2, half, feats)
    lens = passage_len[None, :].astype(F32)
    passages = gather({0: passage_out}, high_bits)
    passages[1] = over_train(after(passage_out, lens), 1)
    query_near = over_train(after(query_out, lens), near)
    passage_y = passages[1].reshape(2, half, feats)

    def half_of(blocks, which):
        return jnp.concatenate(
            [lax.dynamic_index_in_dim(b, which, 0, keepdims=False) for b in blocks], axis=0
        )

    factors = jnp.concatenate(
        (
            dot(proj_in, after(query_in, lens), 0, 1),
            dot(proj_in, after(passage_in_sum, lens), 0, 1),
            dot(proj_out, after(query_out, lens), 0, 1),
            dot(proj_out, after(passage_out, lens), 0, 1),
        ),
        axis=0,
    )
    bit = 1
    while bit < n_test:
        factors = factors + over_test(factors, bit)
        bit *= 2

    def over_cores(blocks, queries):
        sent = over_test(dot(half_of(blocks, 1 - core), queries, 1, 1), 1)
        return dot(half_of(blocks, core), queries, 1, 1) + sent

    def over_chips(total):
        width = total.shape[1]
        bit = n_test // 2
        while bit > 1:
            width //= 2
            upper = lax.rem(lax.div(me_test, bit), 2)
            keep = lax.dynamic_slice_in_dim(total, upper * width, width, 1)
            give = lax.dynamic_slice_in_dim(total, (1 - upper) * width, width, 1)
            total = keep + over_test(give, bit)
            bit //= 2
        return total

    first = [halves, passage_y]
    own_part = over_cores(first, query_out)
    tests_y = over_train(after(test_grads, passages[1]), 1)
    small = lax.dynamic_slice_in_dim(after(factors, own_part)[3 * rank :], core * half, half, 1)
    small_y = over_train(small, 1)
    for mask in masks:
        if mask & 1 and mask & ~1:
            passages[mask] = over_train(after(passages[mask & ~1], tests_y), 1)

    own_part = over_chips(own_part)
    query_near = after(query_near, small_y, own_part)
    queries = jnp.stack((query_out, query_near)).reshape(2, segs, seg, feats)
    queries = queries.transpose(1, 0, 2, 3).reshape(2 * rows, feats)
    near_part = over_chips(over_cores(first, query_near))
    top_part = jnp.concatenate((own_part, near_part), axis=1)
    logits = {0: top_part[:half], 1: top_part[half:]}
    for mask in masks:
        if mask & ~1:
            last_part = over_cores([passages[mask].reshape(2, half, feats)], queries)
            if not mask & 1:
                mid_part = last_part
            logits[mask] = over_chips(last_part)
    logits = jnp.concatenate([logits[mask] for mask in masks], axis=0) * scale

    pass_small = jnp.concatenate((small, small_y), axis=1)
    pass_small = gather({0: after(pass_small, mid_part)}, high_bits)
    pass_small = jnp.concatenate(
        [pass_small[m & ~1][:, (m & 1) * half : (m & 1) * half + half] for m in masks], axis=1
    )
    shared = jnp.concatenate(
        (
            factors[:rank],
            factors[rank : 2 * rank] / lens,
            factors[2 * rank : 3 * rank],
            jnp.broadcast_to(positive[None, :].astype(F32), (8, rows)),
        ),
        axis=0,
    )
    shared_near = over_train(after(shared, mid_part), near)
    mine_of = jnp.concatenate(
        [
            lax.dynamic_slice_in_dim(a[2 * rank :], seg_at * seg, seg, 1)
            for a in (shared, shared_near)
        ],
        axis=1,
    )
    query_small, wanted = mine_of[:rank], mine_of[rank : rank + 1]

    def swap(a):
        return jnp.concatenate((a[:, seg:], a[:, :seg]), axis=1)

    logits = after(logits, pass_small, shared_near)
    top = jnp.max(logits, axis=0, keepdims=True)
    total = jnp.sum(jnp.exp(logits - top), axis=0, keepdims=True)

    def merge(top, total, other):
        new_top = jnp.maximum(top, other[:1])
        return new_top, total * jnp.exp(top - new_top) + other[1:] * jnp.exp(other[:1] - new_top)

    top, total = merge(top, total, over_test(jnp.concatenate((top, total), axis=0), 1))
    top, total = merge(
        top, total, over_train(swap(jnp.concatenate((top, total), axis=0)), near)
    )
    columns = jnp.concatenate(
        [
            lax.broadcasted_iota(jnp.int32, (half, 1), 0)
            + ((me_train ^ mask) * rows + core * half)
            for mask in masks
        ],
        axis=0,
    )
    prob = jnp.exp(logits - top) / total
    dlogit = (prob - (columns == wanted.astype(jnp.int32)).astype(F32)).astype(BF16)

    out_query = dot(split_two(pass_small), dlogit, 1, 0)
    out_query = (out_query[:rank] + out_query[rank:]) * scale
    out_pass = dot(split_two(query_small), dlogit, 1, 1)
    out_pass = (out_pass[:rank] + out_pass[rank:]) * scale

    for bit in reversed(far):
        width = out_pass.shape[1] // 2
        out_pass = out_pass[:, :width] + over_train(out_pass[:, width:], bit)
        if bit == 1:
            out_pass_y = out_pass
    bit = 2
    while bit < n_test:
        out_pass = out_pass + over_test(out_pass, bit)
        bit *= 2
    out_pass = jnp.concatenate((out_pass, over_train(out_pass, near)), axis=0)
    out_pass_other = over_test(out_pass, 1)
    out_pass = jnp.where(
        core == 0,
        jnp.concatenate((out_pass, out_pass_other), axis=1),
        jnp.concatenate((out_pass_other, out_pass), axis=1),
    )

    out_query = out_query + over_test(out_query, 1)
    out_query = out_query + over_train(swap(out_query), near)
    out_query = jnp.concatenate((out_query[:, :seg], out_query[:, seg:]), axis=0)
    bit = 2
    while bit < n_test:
        other = over_test(out_query, bit)
        out_query = jnp.where(
            lax.rem(lax.div(me_test, bit), 2) == 0,
            jnp.concatenate((out_query, other), axis=1),
            jnp.concatenate((other, out_query), axis=1),
        )
        bit *= 2

    held = gather({0: after(test_grads, mid_part)}, high_bits)
    held = {m: after(a, out_pass_y) if m else a for m, a in held.items()}
    held.update({m | 1: over_train(a, 1) if m else tests_y for m, a in held.items()})
    test_block = jnp.zeros((n_far * tests, test_grads.shape[1]), BF16)
    for mask in masks:
        owner = me_train ^ mask
        at = lax.div(owner, 2 * near) * near + lax.rem(owner, near)
        test_block = lax.dynamic_update_slice_in_dim(test_block, held[mask], at * tests, 0)

    def scores_of(acts, which):
        oq = out_query[which * rank : (which + 1) * rank]
        op = out_pass[which * rank : (which + 1) * rank]
        outer = (
            acts[:rank][:, None, :] * oq[None, :, :]
            + acts[rank : 2 * rank][:, None, :] * op[None, :, :]
        )
        grads = outer.reshape(rank * rank, rows).astype(BF16)
        return dot(grads, test_block, 0, 1)

    given = over_train(scores_of(shared_near, 1).astype(BF16), near).astype(F32)
    mine = scores_of(shared, 0)
    unit = near * tests
    mine = [mine[:, i : i + unit] for i in range(0, mine.shape[1], unit)]
    given = [given[:, i : i + unit] for i in range(0, given.shape[1], unit)]
    upper = lax.rem(lax.div(me_train, near), 2) == 1
    pieces = []
    for a, b in zip(mine, given):
        pieces += [jnp.where(upper, b, a), jnp.where(upper, a, b)]
    return jnp.concatenate(pieces, axis=1)


def solution(mesh):
    def body(*args):
        return local(mesh.shape["train"], mesh.shape["test"], *args)

    return jax.shard_map(
        body,
        mesh=mesh,
        in_specs=(
            P("train", "test"),
            P("train", "test"),
            P("train", "test"),
            P("train", "test"),
            P("train"),
            P("train"),
            P("test", None),
            P("test", None),
            P(("test", "train"), None),
        ),
        out_specs=P("train", "test"),
        check_vma=False,
    )
```

```python
import math

import jax
import jax.numpy as jnp
from jax import lax
from jax.sharding import PartitionSpec as P

D = 3584
F32 = jnp.float32
BF16 = jnp.bfloat16


def dot(a, b, ca, cb):
    return lax.dot_general(a, b, (((ca,), (cb,)), ((), ())), preferred_element_type=F32)


def split_two(a):
    high = lax.reduce_precision(a, exponent_bits=8, mantissa_bits=7)
    return jnp.concatenate((high.astype(BF16), (a - high).astype(BF16)), axis=0)


def after(a, *others):
    return lax.optimization_barrier((a, *others))[0]


def local(
    n_train,
    n_test,
    query_out,
    query_in,
    passage_out,
    passage_in_sum,
    passage_len,
    positive,
    proj_in,
    proj_out,
    test_grads,
):
    rank = proj_in.shape[1]
    rows, feats = query_out.shape
    tests = test_grads.shape[0]
    scale = 1.0 / math.sqrt(D)
    me_train = lax.axis_index("train")
    me_test = lax.axis_index("test")
    core = lax.rem(me_test, 2)
    seg_at = lax.div(me_test, 2)
    segs = n_test // 2
    seg = rows // segs
    half = rows // 2
    near = 2
    high_bits = [1 << i for i in range(2, n_train.bit_length() - 1)]
    far = high_bits + [1]

    def over_train(a, bit):
        return lax.ppermute(a, "train", [(i, i ^ bit) for i in range(n_train)])

    def over_test(a, bit):
        return lax.ppermute(a, "test", [(i, i ^ bit) for i in range(n_test)])

    def gather(held, bits):
        held = dict(held)
        for bit in reversed(bits):
            held.update({mask | bit: over_train(a, bit) for mask, a in list(held.items())})
        return held

    masks = [0]
    for bit in far:
        masks = masks + [mask | bit for mask in masks]
    n_far = len(masks)

    halves = passage_out.reshape(2, half, feats)
    lens = passage_len[None, :].astype(F32)
    passages = gather({0: passage_out}, high_bits)
    passages[1] = over_train(after(passage_out, lens), 1)
    query_near = over_train(after(query_out, lens), near)
    passage_y = passages[1].reshape(2, half, feats)

    def half_of(blocks, which):
        return jnp.concatenate(
            [lax.dynamic_index_in_dim(b, which, 0, keepdims=False) for b in blocks], axis=0
        )

    factors = jnp.concatenate(
        (
            dot(proj_in, after(query_in, lens), 0, 1),
            dot(proj_in, after(passage_in_sum, lens), 0, 1),
            dot(proj_out, after(query_out, lens), 0, 1),
            dot(proj_out, after(passage_out, lens), 0, 1),
        ),
        axis=0,
    )
    bit = 1
    while bit < n_test:
        factors = factors + over_test(factors, bit)
        bit *= 2

    def over_cores(blocks, queries):
        sent = over_test(dot(half_of(blocks, 1 - core), queries, 1, 1), 1)
        return dot(half_of(blocks, core), queries, 1, 1) + sent

    def over_chips(total):
        width = total.shape[1]
        bit = n_test // 2
        while bit > 1:
            width //= 2
            upper = lax.rem(lax.div(me_test, bit), 2)
            keep = lax.dynamic_slice_in_dim(total, upper * width, width, 1)
            give = lax.dynamic_slice_in_dim(total, (1 - upper) * width, width, 1)
            total = keep + over_test(give, bit)
            bit //= 2
        return total

    first = [halves, passage_y]
    own_part = over_cores(first, query_out)
    tests_y = over_train(after(test_grads[:32], passages[1]), 1)
    small = lax.dynamic_slice_in_dim(after(factors, own_part)[3 * rank :], core * half, half, 1)
    small_y = over_train(small, 1)
    for mask in masks:
        if mask & 1 and mask & ~1:
            passages[mask] = over_train(after(passages[mask & ~1], own_part, tests_y), 1)

    own_part = over_chips(own_part)
    query_near = after(query_near, small_y)
    queries = jnp.stack((query_out, query_near)).reshape(2, segs, seg, feats)
    queries = queries.transpose(1, 0, 2, 3).reshape(2 * rows, feats)
    near_part = over_chips(over_cores(first, query_near))
    top_part = jnp.concatenate((own_part, near_part), axis=1)
    logits = {0: top_part[:half], 1: top_part[half:]}
    for mask in masks:
        if mask & ~1:
            last_part = over_cores([passages[mask].reshape(2, half, feats)], queries)
            if not mask & 1:
                mid_part = last_part
            logits[mask] = over_chips(last_part)
    logits = jnp.concatenate([logits[mask] for mask in masks], axis=0) * scale

    pass_small = jnp.concatenate((small, small_y), axis=1)
    pass_small = gather({0: after(pass_small, mid_part)}, high_bits)
    pass_small = jnp.concatenate(
        [pass_small[m & ~1][:, (m & 1) * half : (m & 1) * half + half] for m in masks], axis=1
    )
    shared = jnp.concatenate(
        (
            factors[:rank],
            factors[rank : 2 * rank] / lens,
            factors[2 * rank : 3 * rank],
            jnp.broadcast_to(positive[None, :].astype(F32), (8, rows)),
        ),
        axis=0,
    )
    shared_near = over_train(after(shared, mid_part), near)
    mine_of = jnp.concatenate(
        [
            lax.dynamic_slice_in_dim(a[2 * rank :], seg_at * seg, seg, 1)
            for a in (shared, shared_near)
        ],
        axis=1,
    )
    query_small, wanted = mine_of[:rank], mine_of[rank : rank + 1]

    def swap(a):
        return jnp.concatenate((a[:, seg:], a[:, :seg]), axis=1)

    tests_y2 = over_train(after(test_grads[32:], *(passages[m] for m in masks if m & 1 and m > 1)), 1)
    tests_y = jnp.concatenate((tests_y, tests_y2), axis=0)
    logits = after(logits, pass_small, shared_near)
    top = jnp.max(logits, axis=0, keepdims=True)
    total = jnp.sum(jnp.exp(logits - top), axis=0, keepdims=True)

    def merge(top, total, other):
        new_top = jnp.maximum(top, other[:1])
        return new_top, total * jnp.exp(top - new_top) + other[1:] * jnp.exp(other[:1] - new_top)

    top, total = merge(top, total, over_test(jnp.concatenate((top, total), axis=0), 1))
    top, total = merge(
        top, total, over_train(after(swap(jnp.concatenate((top, total), axis=0)), tests_y2), near)
    )
    columns = jnp.concatenate(
        [
            lax.broadcasted_iota(jnp.int32, (half, 1), 0)
            + ((me_train ^ mask) * rows + core * half)
            for mask in masks
        ],
        axis=0,
    )
    prob = jnp.exp(logits - top) / total
    dlogit = (prob - (columns == wanted.astype(jnp.int32)).astype(F32)).astype(BF16)

    out_query = dot(split_two(pass_small), dlogit, 1, 0)
    out_query = (out_query[:rank] + out_query[rank:]) * scale
    out_pass = dot(split_two(query_small), dlogit, 1, 1)
    out_pass = (out_pass[:rank] + out_pass[rank:]) * scale

    for bit in reversed(far):
        width = out_pass.shape[1] // 2
        out_pass = out_pass[:, :width] + over_train(out_pass[:, width:], bit)
        if bit == 1:
            out_pass_y = out_pass
    bit = 2
    while bit < n_test:
        out_pass = out_pass + over_test(out_pass, bit)
        bit *= 2
    out_pass = jnp.concatenate((out_pass, over_train(out_pass, near)), axis=0)
    out_pass_other = over_test(out_pass, 1)
    out_pass = jnp.where(
        core == 0,
        jnp.concatenate((out_pass, out_pass_other), axis=1),
        jnp.concatenate((out_pass_other, out_pass), axis=1),
    )

    out_query = out_query + over_test(out_query, 1)
    out_query = out_query + over_train(swap(out_query), near)
    out_query = jnp.concatenate((out_query[:, :seg], out_query[:, seg:]), axis=0)
    bit = 2
    while bit < n_test:
        other = over_test(out_query, bit)
        out_query = jnp.where(
            lax.rem(lax.div(me_test, bit), 2) == 0,
            jnp.concatenate((out_query, other), axis=1),
            jnp.concatenate((other, out_query), axis=1),
        )
        bit *= 2

    held = gather({0: after(test_grads, mid_part)}, high_bits)
    held = {m: after(a, out_pass_y) if m else a for m, a in held.items()}
    held.update({m | 1: over_train(a, 1) if m else tests_y for m, a in held.items()})
    test_block = jnp.zeros((n_far * tests, test_grads.shape[1]), BF16)
    for mask in masks:
        owner = me_train ^ mask
        at = lax.div(owner, 2 * near) * near + lax.rem(owner, near)
        test_block = lax.dynamic_update_slice_in_dim(test_block, held[mask], at * tests, 0)

    def scores_of(acts, which):
        oq = out_query[which * rank : (which + 1) * rank]
        op = out_pass[which * rank : (which + 1) * rank]
        outer = (
            acts[:rank][:, None, :] * oq[None, :, :]
            + acts[rank : 2 * rank][:, None, :] * op[None, :, :]
        )
        grads = outer.reshape(rank * rank, rows).astype(BF16)
        return dot(grads, test_block, 0, 1)

    given = over_train(scores_of(shared_near, 1).astype(BF16), near).astype(F32)
    mine = scores_of(shared, 0)
    unit = near * tests
    mine = [mine[:, i : i + unit] for i in range(0, mine.shape[1], unit)]
    given = [given[:, i : i + unit] for i in range(0, given.shape[1], unit)]
    upper = lax.rem(lax.div(me_train, near), 2) == 1
    pieces = []
    for a, b in zip(mine, given):
        pieces += [jnp.where(upper, b, a), jnp.where(upper, a, b)]
    return jnp.concatenate(pieces, axis=1)


def solution(mesh):
    def body(*args):
        return local(mesh.shape["train"], mesh.shape["test"], *args)

    return jax.shard_map(
        body,
        mesh=mesh,
        in_specs=(
            P("train", "test"),
            P("train", "test"),
            P("train", "test"),
            P("train", "test"),
            P("train"),
            P("train"),
            P("test", None),
            P("test", None),
            P(("test", "train"), None),
        ),
        out_specs=P("train", "test"),
        check_vma=False,
    )
```

```python
import math

import jax
import jax.numpy as jnp
from jax import lax
from jax.sharding import PartitionSpec as P

D = 3584
F32 = jnp.float32
BF16 = jnp.bfloat16


def dot(a, b, ca, cb):
    return lax.dot_general(a, b, (((ca,), (cb,)), ((), ())), preferred_element_type=F32)


def split_two(a):
    high = lax.reduce_precision(a, exponent_bits=8, mantissa_bits=7)
    return jnp.concatenate((high.astype(BF16), (a - high).astype(BF16)), axis=0)


def after(a, *others):
    return lax.optimization_barrier((a, *others))[0]


def local(
    n_train,
    n_test,
    query_out,
    query_in,
    passage_out,
    passage_in_sum,
    passage_len,
    positive,
    proj_in,
    proj_out,
    test_grads,
):
    rank = proj_in.shape[1]
    rows, feats = query_out.shape
    tests = test_grads.shape[0]
    scale = 1.0 / math.sqrt(D)
    me_train = lax.axis_index("train")
    me_test = lax.axis_index("test")
    core = lax.rem(me_test, 2)
    seg_at = lax.div(me_test, 2)
    segs = n_test // 2
    seg = rows // segs
    half = rows // 2
    near = 2
    high_bits = [1 << i for i in range(2, n_train.bit_length() - 1)]
    far = high_bits + [1]

    def over_train(a, bit):
        return lax.ppermute(a, "train", [(i, i ^ bit) for i in range(n_train)])

    def over_test(a, bit):
        return lax.ppermute(a, "test", [(i, i ^ bit) for i in range(n_test)])

    def gather(held, bits):
        held = dict(held)
        for bit in reversed(bits):
            held.update({mask | bit: over_train(a, bit) for mask, a in list(held.items())})
        return held

    masks = [0]
    for bit in far:
        masks = masks + [mask | bit for mask in masks]
    n_far = len(masks)

    halves = passage_out.reshape(2, half, feats)
    lens = passage_len[None, :].astype(F32)
    passages = gather({0: passage_out}, high_bits)
    passages[1] = over_train(after(passage_out, lens), 1)
    query_near = over_train(after(query_out, lens), near)
    passage_y = passages[1].reshape(2, half, feats)

    def half_of(blocks, which):
        return jnp.concatenate(
            [lax.dynamic_index_in_dim(b, which, 0, keepdims=False) for b in blocks], axis=0
        )

    factors = jnp.concatenate(
        (
            dot(proj_in, after(query_in, lens), 0, 1),
            dot(proj_in, after(passage_in_sum, lens), 0, 1),
            dot(proj_out, after(query_out, lens), 0, 1),
            dot(proj_out, after(passage_out, lens), 0, 1),
        ),
        axis=0,
    )
    bit = 1
    while bit < n_test:
        factors = factors + over_test(factors, bit)
        bit *= 2

    def over_cores(blocks, queries):
        sent = over_test(dot(half_of(blocks, 1 - core), queries, 1, 1), 1)
        return dot(half_of(blocks, core), queries, 1, 1) + sent

    def over_chips(total):
        width = total.shape[1]
        bit = n_test // 2
        while bit > 1:
            width //= 2
            upper = lax.rem(lax.div(me_test, bit), 2)
            keep = lax.dynamic_slice_in_dim(total, upper * width, width, 1)
            give = lax.dynamic_slice_in_dim(total, (1 - upper) * width, width, 1)
            total = keep + over_test(give, bit)
            bit //= 2
        return total

    tests_cut = tests // 2
    tests_y = over_train(test_grads[:tests_cut], 1)
    tests_y1 = tests_y
    small = lax.dynamic_slice_in_dim(after(factors, tests_y1)[3 * rank :], core * half, half, 1)
    small_y = over_train(small, 1)
    pass_high = tuple(passages[m] for m in masks if m > 1 and not m & 1)
    for mask in masks:
        if mask & 1 and mask & ~1:
            passages[mask] = over_train(after(passages[mask & ~1], factors, tests_y1), 1)
    pass_far = tuple(passages[m] for m in masks if m > 1 and m & 1)
    early = [0, 1] + [m for m in masks if m > 1 and not m & 1]
    first = [halves, passage_y] + [passages[m].reshape(2, half, feats) for m in early[2:]]
    own_core = own_part = over_cores(first, after(query_out, factors, tests_y1))

    own_part = over_chips(after(own_part, factors))
    queries = jnp.stack((query_out, query_near)).reshape(2, segs, seg, feats)
    queries = queries.transpose(1, 0, 2, 3).reshape(2 * rows, feats)
    near_core = over_cores(first, query_near)
    near_part = over_chips(near_core)
    top_part = jnp.concatenate((own_part, near_part), axis=1)
    logits = {m: top_part[i * half : (i + 1) * half] for i, m in enumerate(early)}
    for mask in masks:
        if mask not in early:
            block = passages[mask]
            last_part = over_cores([block.reshape(2, half, feats)], queries)
            logits[mask] = over_chips(last_part)
    logits = jnp.concatenate([logits[mask] for mask in masks], axis=0) * scale

    pass_small = jnp.concatenate((small, small_y), axis=1)
    pass_small = gather({0: after(pass_small, near_core)}, high_bits)
    pass_small = jnp.concatenate(
        [pass_small[m & ~1][:, (m & 1) * half : (m & 1) * half + half] for m in masks], axis=1
    )
    shared = jnp.concatenate(
        (
            factors[:rank],
            factors[rank : 2 * rank] / lens,
            factors[2 * rank : 3 * rank],
            jnp.broadcast_to(positive[None, :].astype(F32), (8, rows)),
        ),
        axis=0,
    )
    shared_near = over_train(after(shared, near_core), near)
    mine_of = jnp.concatenate(
        [
            lax.dynamic_slice_in_dim(a[2 * rank :], seg_at * seg, seg, 1)
            for a in (shared, shared_near)
        ],
        axis=1,
    )
    query_small, wanted = mine_of[:rank], mine_of[rank : rank + 1]

    def swap(a):
        return jnp.concatenate((a[:, seg:], a[:, :seg]), axis=1)

    tests_y2 = over_train(after(test_grads[tests_cut:], *pass_far), 1)
    tests_y = jnp.concatenate((tests_y, tests_y2), axis=0)
    top = jnp.max(logits, axis=0, keepdims=True)
    total = jnp.sum(jnp.exp(logits - top), axis=0, keepdims=True)

    def merge(top, total, other):
        new_top = jnp.maximum(top, other[:1])
        return new_top, total * jnp.exp(top - new_top) + other[1:] * jnp.exp(other[:1] - new_top)

    top, total = merge(top, total, over_test(jnp.concatenate((top, total), axis=0), 1))
    top, total = merge(
        top, total, over_train(after(swap(jnp.concatenate((top, total), axis=0)), tests_y2, pass_small), near)
    )
    columns = jnp.concatenate(
        [
            lax.broadcasted_iota(jnp.int32, (half, 1), 0)
            + ((me_train ^ mask) * rows + core * half)
            for mask in masks
        ],
        axis=0,
    )
    prob = jnp.exp(logits - top) / total
    dlogit = (prob - (columns == wanted.astype(jnp.int32)).astype(F32)).astype(BF16)

    dlogit = after(dlogit, tests_y2)

    out_query = dot(split_two(pass_small), dlogit, 1, 0)
    out_query = (out_query[:rank] + out_query[rank:]) * scale
    out_pass = dot(split_two(query_small), dlogit, 1, 1)
    out_pass = (out_pass[:rank] + out_pass[rank:]) * scale

    for bit in reversed(far):
        width = out_pass.shape[1] // 2
        out_pass = out_pass[:, :width] + over_train(out_pass[:, width:], bit)
        if bit == 1:
            out_pass_y = out_pass
    out_pass_z = out_pass
    bit = 2
    while bit < n_test:
        out_pass = out_pass + over_test(out_pass, bit)
        bit *= 2
    out_pass = jnp.concatenate((out_pass, over_train(out_pass, near)), axis=0)
    out_pass_other = over_test(out_pass, 1)
    out_pass = jnp.where(
        core == 0,
        jnp.concatenate((out_pass, out_pass_other), axis=1),
        jnp.concatenate((out_pass_other, out_pass), axis=1),
    )

    out_query = out_query + over_test(out_query, 1)
    out_query = out_query + over_train(swap(out_query), near)
    out_query = jnp.concatenate((out_query[:, :seg], out_query[:, seg:]), axis=0)
    bit = 2
    while bit < n_test:
        other = over_test(out_query, bit)
        out_query = jnp.where(
            lax.rem(lax.div(me_test, bit), 2) == 0,
            jnp.concatenate((out_query, other), axis=1),
            jnp.concatenate((other, out_query), axis=1),
        )
        bit *= 2

    held = gather({0: after(test_grads, near_core)}, high_bits)
    held = {m: after(a, tests_y2, out_pass_y) if m else a for m, a in held.items()}
    held.update({m | 1: over_train(a, 1) if m else tests_y for m, a in held.items()})
    test_block = jnp.zeros((n_far * tests, test_grads.shape[1]), BF16)
    for mask in masks:
        owner = me_train ^ mask
        at = lax.div(owner, 2 * near) * near + lax.rem(owner, near)
        test_block = lax.dynamic_update_slice_in_dim(test_block, held[mask], at * tests, 0)

    def scores_of(acts, which, out_query):
        oq = out_query[which * rank : (which + 1) * rank]
        op = out_pass[which * rank : (which + 1) * rank]
        outer = (
            acts[:rank][:, None, :] * oq[None, :, :]
            + acts[rank : 2 * rank][:, None, :] * op[None, :, :]
        )
        grads = outer.reshape(rank * rank, rows).astype(BF16)
        return dot(grads, test_block, 0, 1)

    scores_near = scores_of(shared_near, 1, out_query).astype(BF16)
    given = over_train(scores_near, near).astype(F32)
    mine = scores_of(shared, 0, out_query)
    unit = near * tests
    mine = [mine[:, i : i + unit] for i in range(0, mine.shape[1], unit)]
    given = [given[:, i : i + unit] for i in range(0, given.shape[1], unit)]
    upper = lax.rem(lax.div(me_train, near), 2) == 1
    pieces = []
    for a, b in zip(mine, given):
        pieces += [jnp.where(upper, b, a), jnp.where(upper, a, b)]
    return jnp.concatenate(pieces, axis=1)


def solution(mesh):
    def body(*args):
        return local(mesh.shape["train"], mesh.shape["test"], *args)

    return jax.shard_map(
        body,
        mesh=mesh,
        in_specs=(
            P("train", "test"),
            P("train", "test"),
            P("train", "test"),
            P("train", "test"),
            P("train"),
            P("train"),
            P("test", None),
            P("test", None),
            P(("test", "train"), None),
        ),
        out_specs=P("train", "test"),
        check_vma=False,
    )
```

```python
import math

import jax
import jax.numpy as jnp
from jax import lax
from jax.sharding import PartitionSpec as P

D = 3584
F32 = jnp.float32
BF16 = jnp.bfloat16


def dot(a, b, ca, cb):
    return lax.dot_general(a, b, (((ca,), (cb,)), ((), ())), preferred_element_type=F32)


def split_two(a):
    high = lax.reduce_precision(a, exponent_bits=8, mantissa_bits=7)
    return jnp.concatenate((high.astype(BF16), (a - high).astype(BF16)), axis=0)


def after(a, *others):
    return lax.optimization_barrier((a, *others))[0]


def local(
    n_train,
    n_test,
    query_out,
    query_in,
    passage_out,
    passage_in_sum,
    passage_len,
    positive,
    proj_in,
    proj_out,
    test_grads,
):
    rank = proj_in.shape[1]
    rows, feats = query_out.shape
    tests = test_grads.shape[0]
    scale = 1.0 / math.sqrt(D)
    me_train = lax.axis_index("train")
    me_test = lax.axis_index("test")
    core = lax.rem(me_test, 2)
    seg_at = lax.div(me_test, 2)
    segs = n_test // 2
    seg = rows // segs
    half = rows // 2
    near = 2
    high_bits = [1 << i for i in range(2, n_train.bit_length() - 1)]
    far = high_bits + [1]

    def over_train(a, bit):
        return lax.ppermute(a, "train", [(i, i ^ bit) for i in range(n_train)])

    def over_test(a, bit):
        return lax.ppermute(a, "test", [(i, i ^ bit) for i in range(n_test)])

    def gather(held, bits):
        held = dict(held)
        for bit in reversed(bits):
            held.update({mask | bit: over_train(a, bit) for mask, a in list(held.items())})
        return held

    masks = [0]
    for bit in far:
        masks = masks + [mask | bit for mask in masks]
    n_far = len(masks)

    halves = passage_out.reshape(2, half, feats)
    lens = passage_len[None, :].astype(F32)
    passages = gather({0: passage_out}, high_bits)
    passages[1] = over_train(after(passage_out, lens), 1)
    query_near = over_train(after(query_out, lens), near)
    passage_y = passages[1].reshape(2, half, feats)

    def half_of(blocks, which):
        return jnp.concatenate(
            [lax.dynamic_index_in_dim(b, which, 0, keepdims=False) for b in blocks], axis=0
        )

    factors = jnp.concatenate(
        (
            dot(proj_in, after(query_in, lens), 0, 1),
            dot(proj_in, after(passage_in_sum, lens), 0, 1),
            dot(proj_out, after(query_out, lens), 0, 1),
            dot(proj_out, after(passage_out, lens), 0, 1),
        ),
        axis=0,
    )
    bit = 1
    while bit < n_test:
        factors = factors + over_test(factors, bit)
        bit *= 2

    def over_cores(blocks, queries):
        sent = over_test(dot(half_of(blocks, 1 - core), queries, 1, 1), 1)
        return dot(half_of(blocks, core), queries, 1, 1) + sent

    def over_chips(total):
        width = total.shape[1]
        bit = n_test // 2
        while bit > 1:
            width //= 2
            upper = lax.rem(lax.div(me_test, bit), 2)
            keep = lax.dynamic_slice_in_dim(total, upper * width, width, 1)
            give = lax.dynamic_slice_in_dim(total, (1 - upper) * width, width, 1)
            total = keep + over_test(give, bit)
            bit //= 2
        return total

    tests_cut = tests // 2
    tests_y = over_train(test_grads[:tests_cut], 1)
    tests_y1 = tests_y
    small = lax.dynamic_slice_in_dim(after(factors, tests_y1)[3 * rank :], core * half, half, 1)
    small_y = over_train(small, 1)
    pass_high = tuple(passages[m] for m in masks if m > 1 and not m & 1)
    for mask in masks:
        if mask & 1 and mask & ~1:
            passages[mask] = over_train(after(passages[mask & ~1], factors, tests_y1), 1)
    pass_far = tuple(passages[m] for m in masks if m > 1 and m & 1)
    early = [0, 1] + [m for m in masks if m > 1 and not m & 1]
    first = [halves, passage_y] + [passages[m].reshape(2, half, feats) for m in early[2:]]
    own_core = own_part = over_cores(first, after(query_out, factors, tests_y1))

    own_part = over_chips(after(own_part, factors))
    queries = jnp.stack((query_out, query_near)).reshape(2, segs, seg, feats)
    queries = queries.transpose(1, 0, 2, 3).reshape(2 * rows, feats)
    near_core = over_cores(first, query_near)
    near_part = over_chips(near_core)
    top_part = jnp.concatenate((own_part, near_part), axis=1)
    logits = {m: top_part[i * half : (i + 1) * half] for i, m in enumerate(early)}
    for mask in masks:
        if mask not in early:
            block = passages[mask]
            last_part = over_cores([block.reshape(2, half, feats)], queries)
            logits[mask] = over_chips(last_part)
    logits = jnp.concatenate([logits[mask] for mask in masks], axis=0) * scale

    pass_small = jnp.concatenate((small, small_y), axis=1)
    pass_small = gather({0: after(pass_small, near_core)}, high_bits)
    pass_small = jnp.concatenate(
        [pass_small[m & ~1][:, (m & 1) * half : (m & 1) * half + half] for m in masks], axis=1
    )
    shared = jnp.concatenate(
        (
            factors[:rank],
            factors[rank : 2 * rank] / lens,
            factors[2 * rank : 3 * rank],
            jnp.broadcast_to(positive[None, :].astype(F32), (8, rows)),
        ),
        axis=0,
    )
    shared_near = over_train(after(shared, near_core), near)
    mine_of = jnp.concatenate(
        [
            lax.dynamic_slice_in_dim(a[2 * rank :], seg_at * seg, seg, 1)
            for a in (shared, shared_near)
        ],
        axis=1,
    )
    query_small, wanted = mine_of[:rank], mine_of[rank : rank + 1]

    def swap(a):
        return jnp.concatenate((a[:, seg:], a[:, :seg]), axis=1)

    tests_y2 = over_train(after(test_grads[tests_cut:], *pass_far), 1)
    tests_y = jnp.concatenate((tests_y, tests_y2), axis=0)
    top = jnp.max(logits, axis=0, keepdims=True)
    total = jnp.sum(jnp.exp(logits - top), axis=0, keepdims=True)

    def merge(top, total, other):
        new_top = jnp.maximum(top, other[:1])
        return new_top, total * jnp.exp(top - new_top) + other[1:] * jnp.exp(other[:1] - new_top)

    top, total = merge(top, total, over_test(jnp.concatenate((top, total), axis=0), 1))
    top, total = merge(
        top, total, over_train(after(swap(jnp.concatenate((top, total), axis=0)), tests_y2, pass_small), near)
    )
    columns = jnp.concatenate(
        [
            lax.broadcasted_iota(jnp.int32, (half, 1), 0)
            + ((me_train ^ mask) * rows + core * half)
            for mask in masks
        ],
        axis=0,
    )
    prob = jnp.exp(logits - top) / total
    dlogit = (prob - (columns == wanted.astype(jnp.int32)).astype(F32)).astype(BF16)

    dlogit = after(dlogit, tests_y2)

    out_query = dot(split_two(pass_small), dlogit, 1, 0)
    out_query = (out_query[:rank] + out_query[rank:]) * scale
    out_pass = dot(split_two(query_small), dlogit, 1, 1)
    out_pass = (out_pass[:rank] + out_pass[rank:]) * scale

    for bit in reversed(far):
        width = out_pass.shape[1] // 2
        out_pass = out_pass[:, :width] + over_train(out_pass[:, width:], bit)
        if bit == 1:
            out_pass_y = out_pass
    out_pass_z = out_pass
    bit = 2
    while bit < n_test:
        out_pass = out_pass + over_test(out_pass, bit)
        bit *= 2
    out_pass_near = over_train(out_pass.astype(BF16), near).astype(F32)
    out_pass = jnp.concatenate((out_pass, out_pass_near), axis=0)
    out_pass_other = over_test(out_pass, 1)
    out_pass = jnp.where(
        core == 0,
        jnp.concatenate((out_pass, out_pass_other), axis=1),
        jnp.concatenate((out_pass_other, out_pass), axis=1),
    )

    out_query = out_query + over_test(out_query, 1)
    out_query = out_query + over_train(swap(out_query), near)
    out_query = jnp.concatenate((out_query[:, :seg], out_query[:, seg:]), axis=0)
    bit = 2
    while bit < n_test:
        other = over_test(out_query, bit)
        out_query = jnp.where(
            lax.rem(lax.div(me_test, bit), 2) == 0,
            jnp.concatenate((out_query, other), axis=1),
            jnp.concatenate((other, out_query), axis=1),
        )
        bit *= 2

    held = gather({0: after(test_grads, near_core)}, high_bits)
    held = {m: after(a, tests_y2, out_pass_y) if m else a for m, a in held.items()}
    held.update({m | 1: over_train(a, 1) if m else tests_y for m, a in held.items()})
    test_block = jnp.zeros((n_far * tests, test_grads.shape[1]), BF16)
    for mask in masks:
        owner = me_train ^ mask
        at = lax.div(owner, 2 * near) * near + lax.rem(owner, near)
        test_block = lax.dynamic_update_slice_in_dim(test_block, held[mask], at * tests, 0)

    def scores_of(acts, which, out_query):
        oq = out_query[which * rank : (which + 1) * rank]
        op = out_pass[which * rank : (which + 1) * rank]
        outer = (
            acts[:rank][:, None, :] * oq[None, :, :]
            + acts[rank : 2 * rank][:, None, :] * op[None, :, :]
        )
        grads = outer.reshape(rank * rank, rows).astype(BF16)
        return dot(grads, test_block, 0, 1)

    scores_near = scores_of(shared_near, 1, out_query).astype(BF16)
    given = over_train(scores_near, near).astype(F32)
    mine = scores_of(shared, 0, out_query)
    unit = near * tests
    mine = [mine[:, i : i + unit] for i in range(0, mine.shape[1], unit)]
    given = [given[:, i : i + unit] for i in range(0, given.shape[1], unit)]
    upper = lax.rem(lax.div(me_train, near), 2) == 1
    pieces = []
    for a, b in zip(mine, given):
        pieces += [jnp.where(upper, b, a), jnp.where(upper, a, b)]
    return jnp.concatenate(pieces, axis=1)


def solution(mesh):
    def body(*args):
        return local(mesh.shape["train"], mesh.shape["test"], *args)

    return jax.shard_map(
        body,
        mesh=mesh,
        in_specs=(
            P("train", "test"),
            P("train", "test"),
            P("train", "test"),
            P("train", "test"),
            P("train"),
            P("train"),
            P("test", None),
            P("test", None),
            P(("test", "train"), None),
        ),
        out_specs=P("train", "test"),
        check_vma=False,
    )
```
